32 devices in a mesh: group: 2 (over x), chan: 16 (over z, y, core).
Axes of the slice: x: 2, y: 2, z: 4, core: 2. Of those that a mesh axis runs over, the one named last changes fastest.
Arguments:
- records: bfloat16 [4, 4096, 2048], P(None, ('group', 'chan')), parts along dimension 1, may hold values from -6 to 6
- dead: int32 [4096], P(('group', 'chan')), parts along dimension 0, may hold values 0 or 1
- glitch: int32 [4, 4096], P(None, ('group', 'chan')), parts along dimension 1, may hold values 0 or 1
- pairs: int32 [512, 2], P(('group', 'chan')), parts along dimension 0, may hold values from -1 to 15, as said below
Outputs:
- stacks: float32 [512, 128, 512], P(('group', 'chan')), parts along dimension 0
The draws below stay inside these ranges and needn't reach their ends.
There are 2 independent parts, one for each index of `group`. The reference program is written for one: setup_inputs(seed, part) draws one part's arguments, and reference() takes and returns one part's arrays. A program takes and returns all parts, laid end to end along the dimension named above; each array names one. Nothing has to cross between parts.
Inputs may be any that keep to these rules, and one draw needn't show every extreme that they name: `pairs`: per row both entries are -1 or both are blocks of the fibre within 4 blocks of the row's owner block; each owner's first slot is filled, and distance 4 is reached.
All inputs are finite; a program needn't handle non-finite values. No bound on the sum of `dead` or of `glitch` on one device may be relied on, other than what follows from the above.
Results may differ from the reference program's by a relative error of at most 0.0042.
Values may be sent and summed in bfloat16 or wider, within the bound.
No kernel may reach another device: no remote copies, remote signals or barrier semaphores. Data moves between devices by JAX's collectives and lax.ppermute only.
A program may use at most 128 MiB of HBM per device.

```python
import math
import jax
import jax.numpy as jnp
from jax import lax

CH = 128
W = 2048
WIN = 4
P_DEV = 16
LAGS = 512
REACH = 4
CHANNELS = 2048
N_CHAN = 16


def draw_pairs(key, part):
    key = jax.random.fold_in(key, 11)
    key_a, key_b, key_c, key_d = jax.random.split(key, 4)
    total = N_CHAN * P_DEV
    index = jnp.arange(total, dtype=jnp.int32)
    owner = index // P_DEV
    slot = index % P_DEV
    first = owner + jax.random.randint(key_a, (total,), -REACH, REACH + 1)
    second = owner + jax.random.randint(key_b, (total,), -REACH, REACH + 1)
    counts = jax.random.randint(key_c, (N_CHAN,), (P_DEV + 1) // 2, P_DEV + 1)
    fullest = jax.random.randint(key_d, (), 0, N_CHAN)
    counts = jnp.where(jnp.arange(N_CHAN, dtype=jnp.int32) == fullest, P_DEV, counts)
    far = jnp.where(owner + REACH < N_CHAN, owner + REACH, owner - REACH)
    first = jnp.where(slot == 0, owner, first)
    second = jnp.where(slot == 0, far, second)
    usable = (first >= 0) & (first < N_CHAN) & (second >= 0) & (second < N_CHAN) & (slot < counts[owner])
    first = jnp.where(usable, first, -1)
    second = jnp.where(usable, second, -1)
    return jnp.stack([first, second], 1).astype(jnp.int32)


def plant(array, own_key, smallest, largest):
    spot = [jax.random.randint(jax.random.fold_in(own_key, axis), (), 0, length) for axis, length in enumerate(array.shape)]
    longest = array.shape.index(max(array.shape))
    beside = spot[:longest] + [(spot[longest] + 1) % array.shape[longest]] + spot[longest + 1:]
    return array.at[tuple(spot)].set(smallest).at[tuple(beside)].set(largest)


def level_of(rng, shape, cuts, low, high):
    def one(axis_at, blocks):
        draws = jax.random.uniform(jax.random.fold_in(jax.random.fold_in(rng, 6), axis_at), (blocks,), jnp.float32, low / len(cuts), high / len(cuts))
        return jnp.repeat(jnp.exp(draws), shape[axis_at] // blocks).reshape((-1,) + (1,) * (len(shape) - axis_at - 1))

    loudness = one(*cuts[0])
    for cut in cuts[1:]:
        loudness = loudness * one(*cut)
    return loudness


def gaussian(rng, extent, scale, reach, shards=(), kind=jnp.bfloat16):
    loudness = level_of(rng, extent, shards, -0.22, 0.18) if shards else 1.0
    result = jax.random.normal(rng, extent, jnp.float32) * scale * loudness
    return jnp.minimum(jnp.maximum(result, -reach), reach).astype(kind)


def setup_inputs(seed: int = 0, part: int = 0) -> dict:
    key_list = jax.random.split(jax.random.key(seed), 5)
    part_splits = jax.random.split(jax.random.fold_in(key_list[4], part), 5)
    return {
        "records": gaussian(part_splits[0], (WIN, CHANNELS, W), 1.0, 6.0, ((1, 16),)),
        "dead": plant((jax.random.randint(part_splits[1], (CHANNELS,), 0, 16) < 15).astype(jnp.int32), jax.random.fold_in(part_splits[1], 1), 0, 1),
        "glitch": plant((jax.random.randint(part_splits[2], (WIN, CHANNELS), 0, 8) < 7).astype(jnp.int32), jax.random.fold_in(part_splits[2], 1), 0, 1),
        "pairs": draw_pairs(jax.random.fold_in(jax.random.fold_in(key_list[4], part), 71), part),
    }


def make_basis(width, bins):
    rows = jnp.arange(width, dtype=jnp.int32)[:, None]
    cols = jnp.arange(bins, dtype=jnp.int32)[None, :] + 1
    phase = (rows * cols % width).astype(jnp.float32) * (2.0 * math.pi / width)
    hann = 0.5 - 0.5 * jnp.cos(jnp.arange(width, dtype=jnp.int32).astype(jnp.float32) * (2.0 * math.pi / width))
    return jnp.concatenate([hann[:, None] * jnp.cos(phase), -hann[:, None] * jnp.sin(phase)], 1).astype(jnp.bfloat16)

def make_lagmap(width, bins, lags):
    rows = jnp.arange(bins, dtype=jnp.int32)[:, None] + 1
    cols = jnp.arange(lags, dtype=jnp.int32)[None, :] - lags // 2 + width
    phase = (rows * cols % width).astype(jnp.float32) * (2.0 * math.pi / width)
    scale = 2.0 / math.sqrt(bins)
    return jnp.concatenate([scale * jnp.cos(phase), -scale * jnp.sin(phase)], 0).astype(jnp.bfloat16)

def whiten(spectra, live, bins):
    real_part = spectra[..., :bins]
    imag_part = spectra[..., bins:]
    amp = jnp.sqrt(real_part * real_part + imag_part * imag_part)
    level = lax.optimization_barrier(jnp.mean(amp, axis=-1, keepdims=True)) + 1e-06
    factor = live[..., None] / (amp + level)
    return jnp.concatenate([real_part * factor, imag_part * factor], -1).astype(jnp.bfloat16)

def cross_pair(left, right, left_live, right_live, bins):
    left = left.astype(jnp.float32)
    right = right.astype(jnp.float32)
    a_re, a_im = (left[..., :bins], left[..., bins:])
    b_re, b_im = (right[..., :bins], right[..., bins:])
    cross_re = lax.optimization_barrier(jnp.sum(a_re * b_re + a_im * b_im, axis=0))
    cross_im = lax.optimization_barrier(jnp.sum(a_re * b_im - a_im * b_re, axis=0))
    count = lax.optimization_barrier(jnp.sum(left_live * right_live, axis=0))
    scale = 1.0 / jnp.maximum(count, 1.0)
    return (jnp.concatenate([cross_re, cross_im], -1) * scale[:, None]).astype(jnp.bfloat16)

def reference(records, dead, glitch, pairs):
    bins = W // 2
    basis = make_basis(W, bins)
    live = dead[None, :].astype(jnp.float32) * glitch.astype(jnp.float32)

    def one_window(args):
        rec, liv = args
        spec = jnp.dot(rec, basis, preferred_element_type=jnp.float32)
        return whiten(spec, liv, bins)
    whitened = lax.map(one_window, (records, live))
    lagmap = make_lagmap(W, bins, LAGS)

    def one_pair(row):
        first, second = (row[0], row[1])
        valid = (first >= 0) & (second >= 0)
        start_a = (jnp.maximum(first, 0) * CH).astype(jnp.int32)
        start_b = (jnp.maximum(second, 0) * CH).astype(jnp.int32)
        left = lax.dynamic_slice_in_dim(whitened, start_a, CH, 1)
        right = lax.dynamic_slice_in_dim(whitened, start_b, CH, 1)
        left_live = lax.dynamic_slice_in_dim(live, start_a, CH, 1)
        right_live = lax.dynamic_slice_in_dim(live, start_b, CH, 1)
        cross = cross_pair(left, right, left_live, right_live, bins)
        cross = jnp.where(valid, cross, jnp.zeros_like(cross))
        return jnp.dot(cross, lagmap, preferred_element_type=jnp.float32)
    return lax.map(one_pair, pairs)
```

```python
import functools
import math

import jax
import jax.numpy as jnp
import numpy as np
from jax import lax
from jax.experimental import pallas as pl
from jax.experimental.pallas import tpu as pltpu
from jax.sharding import PartitionSpec as P

LAGS = 512
QUAD = 4
CHUNKS = (8, 8, 8, 8)


def make_basis(width, bins):
    rows = np.arange(width, dtype=np.int64)[:, None]
    cols = np.arange(bins, dtype=np.int64)[None, :] + 1
    phase = (rows * cols % width) * (2.0 * math.pi / width)
    hann = 0.5 - 0.5 * np.cos(np.arange(width) * (2.0 * math.pi / width))
    table = np.concatenate([hann[:, None] * np.cos(phase), -hann[:, None] * np.sin(phase)], 1)
    return table.astype(np.float32).astype(jnp.bfloat16)


def make_lagmap(width, bins, lags):
    rows = np.arange(bins, dtype=np.int64)[:, None] + 1
    cols = np.arange(lags, dtype=np.int64)[None, :] - lags // 2 + width
    phase = (rows * cols % width) * (2.0 * math.pi / width)
    scale = 2.0 / math.sqrt(bins)
    table = np.concatenate([scale * np.cos(phase), -scale * np.sin(phase)], 0)
    return table.astype(np.float32).astype(jnp.bfloat16)


def to_quad_peer(value, mask):
    count = lax.axis_size("chan")
    return lax.ppermute(value, "chan", [(s, s ^ mask) for s in range(count)])


def to_next_quad(value, steps):
    count = lax.axis_size("chan")
    first, last = max(0, -steps), min(count, count - steps)
    return lax.ppermute(value, "chan", [(s, s + steps) for s in range(first, last)])


def whiten_kernel(x0, x1, x2, x3, live, basis, out, rows, re_s, im_s, amp_s):
    part = x0.shape[0]
    bins = basis.shape[1] // 2
    for m, x in enumerate((x0, x1, x2, x3)):
        rows[pl.ds(m * part, part), :] = x[...]
    step = 256
    total = jnp.zeros((QUAD * part, 128), jnp.float32)
    for j in range(0, bins, step):
        re = jnp.dot(rows[...], basis[:, j : j + step], preferred_element_type=jnp.float32)
        im = jnp.dot(
            rows[...], basis[:, bins + j : bins + j + step], preferred_element_type=jnp.float32
        )
        amp = jnp.sqrt(re * re + im * im)
        re_s[:, j : j + step] = re
        im_s[:, j : j + step] = im
        amp_s[:, j : j + step] = amp
        for i in range(0, step, 128):
            total = total + amp[:, i : i + 128]
    level = jnp.sum(total, axis=-1, keepdims=True) * (1.0 / bins) + 1e-06
    flag = live[:, 0:1]
    for j in range(0, bins, step):
        factor = flag / (amp_s[:, j : j + step] + level)
        out[:, j : j + step] = (re_s[:, j : j + step] * factor).astype(jnp.bfloat16)
        out[:, bins + j : bins + j + step] = (im_s[:, j : j + step] * factor).astype(jnp.bfloat16)


def whiten(parts, live, basis):
    part, width = parts[0].shape
    total = QUAD * part
    bins = width // 2
    return pl.pallas_call(
        whiten_kernel,
        out_shape=jax.ShapeDtypeStruct((total, width), jnp.bfloat16),
        in_specs=[pl.BlockSpec(memory_space=pltpu.VMEM)] * 6,
        out_specs=pl.BlockSpec(memory_space=pltpu.VMEM),
        scratch_shapes=[
            pltpu.VMEM((total, width), jnp.bfloat16),
            pltpu.VMEM((total, bins), jnp.float32),
            pltpu.VMEM((total, bins), jnp.float32),
            pltpu.VMEM((total, bins), jnp.float32),
        ],
        compiler_params=pltpu.CompilerParams(vmem_limit_bytes=24 << 20),
        cost_estimate=pl.CostEstimate(
            flops=2 * total * width * width, bytes_accessed=8 << 20, transcendentals=0
        ),
        name="whiten",
    )(*parts, live, basis)


def cross_kernel(windows, place, valid, behind, mine, ahead, live, lagmap, out, near, cross):
    rows, width = behind.shape
    bins = width // 2
    chans = rows // (QUAD * windows)
    for i, block in enumerate((behind, mine, ahead)):
        near[pl.ds(i * rows, rows), :] = block[...].astype(jnp.float32)
    span = windows * chans
    pairs = place.shape[0]

    def one(p):
        a = pl.multiple_of(place[p, 0] * span, span)
        b = pl.multiple_of(place[p, 1] * span, span)
        count = jnp.zeros((chans, 128), jnp.float32)
        for w in range(windows):
            count = count + live[pl.ds(a + w * chans, chans), :] * live[pl.ds(b + w * chans, chans), :]
        scale = valid[p] * (1.0 / jnp.maximum(count, 1.0))
        res, ims = [], []
        for j in range(0, bins, 128):
            re = jnp.zeros((chans, 128), jnp.float32)
            im = jnp.zeros((chans, 128), jnp.float32)
            for w in range(windows):
                ra = near[pl.ds(a + w * chans, chans), pl.ds(j, 128)]
                ia = near[pl.ds(a + w * chans, chans), pl.ds(bins + j, 128)]
                rb = near[pl.ds(b + w * chans, chans), pl.ds(j, 128)]
                ib = near[pl.ds(b + w * chans, chans), pl.ds(bins + j, 128)]
                re = re + (ra * rb + ia * ib)
                im = im + (ra * ib - ia * rb)
            res.append(re * scale)
            ims.append(im * scale)
        return res + ims

    def two(h, carry):
        first = one(2 * h)
        second = one(2 * h + 1)
        for j, (u, v) in enumerate(zip(first, second)):
            cross[pl.ds(pl.multiple_of(2 * h * chans, 2 * chans), 2 * chans), pl.ds(j * 128, 128)] = (
                jnp.concatenate([u, v], 0).astype(jnp.bfloat16)
            )
        return carry

    lax.fori_loop(0, pairs // 2, two, 0)
    out[...] = jnp.dot(cross[...], lagmap[...], preferred_element_type=jnp.float32).astype(
        jnp.bfloat16
    )


def cross_stack(windows, place, valid, behind, mine, ahead, live, lagmap):
    rows, width = mine.shape
    chans = rows // (QUAD * windows)
    pairs = place.shape[0]

    smem = pl.BlockSpec(memory_space=pltpu.SMEM)
    vmem = pl.BlockSpec(memory_space=pltpu.VMEM)
    return pl.pallas_call(
        functools.partial(cross_kernel, windows),
        out_shape=jax.ShapeDtypeStruct((pairs * chans, LAGS), jnp.bfloat16),
        in_specs=[smem, smem] + [vmem] * 5,
        out_specs=vmem,
        scratch_shapes=[
            pltpu.VMEM((3 * rows, width), jnp.float32),
            pltpu.VMEM((pairs * chans, width), jnp.bfloat16),
        ],
        compiler_params=pltpu.CompilerParams(vmem_limit_bytes=24 << 20),
        cost_estimate=pl.CostEstimate(
            flops=2 * pairs * chans * width * LAGS * 3, bytes_accessed=8 << 20, transcendentals=0
        ),
        name="cross_stack",
    )(place, valid, behind, mine, ahead, live, lagmap)


def place_kernel(chans, slot, r0, r1, r2, r3, *refs):
    out = refs[-1]
    for m, r in enumerate((r0, r1, r2, r3)):
        at = pl.multiple_of(slot[m] * chans, chans)
        for p in range(out.shape[0]):
            out[p, pl.ds(at, chans), :] = r[pl.ds(p * chans, chans), :].astype(jnp.float32)


def place_stacks(chunk, chans, slot, parts, held, shape):

    smem = pl.BlockSpec(memory_space=pltpu.SMEM)
    extra = [] if held is None else [held]
    pairs = shape[0]
    full = lambda i: (0, 0)
    return pl.pallas_call(
        functools.partial(place_kernel, chans),
        out_shape=jax.ShapeDtypeStruct(shape, jnp.float32),
        grid=(1,),
        in_specs=[smem]
        + [pl.BlockSpec((pairs * chans, LAGS), full)] * 4
        + [pl.BlockSpec(memory_space=pl.ANY)] * len(extra),
        out_specs=pl.BlockSpec((pairs, QUAD * chans, LAGS), lambda i: (0, chunk, 0)),
        input_output_aliases={5: 0} if extra else {},
        compiler_params=pltpu.CompilerParams(vmem_limit_bytes=16 << 20),
        cost_estimate=pl.CostEstimate(flops=0, bytes_accessed=2 << 20, transcendentals=0),
        name="place_stacks",
    )(slot, *parts, *extra)


def body(records, dead, glitch, pairs):
    windows, block, width = records.shape
    bins = width // 2
    here = lax.axis_index("chan")
    mine = here % QUAD
    quad = here // QUAD
    basis = jnp.asarray(make_basis(width, bins))
    lagmap = jnp.asarray(make_lagmap(width, bins, LAGS))
    order = [mine ^ m for m in range(QUAD)]

    live = dead[None, :] * glitch
    notes = jnp.concatenate([live.reshape(-1), pairs.reshape(-1)])
    notes = lax.all_gather(notes, "chan")
    all_live = notes[:, : windows * block].reshape(-1, windows, block)
    all_pairs = notes[:, windows * block :].reshape(-1, pairs.shape[0], 2)
    near_live = lax.dynamic_slice_in_dim(
        jnp.pad(all_live, ((QUAD, QUAD), (0, 0), (0, 0))), quad * QUAD, 3 * QUAD, 0
    ).astype(jnp.float32)
    near_live = near_live.reshape(3, QUAD, windows, block)
    near_live = jnp.stack([lax.dynamic_index_in_dim(near_live, o, 1, False) for o in order], 1)
    quad_pairs = jnp.stack(
        [lax.dynamic_index_in_dim(all_pairs, quad * QUAD + o, 0, False) for o in order], 0
    ).reshape(-1, 2)
    valid = ((quad_pairs[:, 0] >= 0) & (quad_pairs[:, 1] >= 0)).astype(jnp.float32)
    place = (quad_pairs // QUAD - quad + 1) * QUAD + ((quad_pairs % QUAD) ^ mine)
    place = jnp.where(valid[:, None] > 0, jnp.clip(place, 0, 3 * QUAD - 1), 0)
    slot = jnp.stack(order)

    held = None
    base = 0
    for chunk, chans in enumerate(CHUNKS):
        sent = records[:, base : base + QUAD * chans, :].reshape(windows, QUAD, chans, width)
        parts = []
        for m in range(QUAD):
            piece = lax.dynamic_index_in_dim(sent, order[m], 1, False).reshape(-1, width)
            parts.append(to_quad_peer(piece, m) if m else piece)
        lives = near_live[..., base : base + QUAD * chans].reshape(3, QUAD, windows, QUAD, chans)
        lives = lax.dynamic_index_in_dim(lives, mine, 3, False).reshape(3, -1, 1)
        lives = jnp.broadcast_to(lives, lives.shape[:2] + (128,))
        white = whiten(parts, lives[1], basis)
        behind = to_next_quad(white, QUAD)
        ahead = to_next_quad(white, -QUAD)
        stacks = cross_stack(
            windows, place, valid, behind, white, ahead, lives.reshape(-1, 128), lagmap
        )
        stacks = stacks.reshape(QUAD, -1, LAGS)
        back = [to_quad_peer(stacks[m], m) if m else stacks[m] for m in range(QUAD)]
        held = place_stacks(chunk, chans, slot, back, held, (pairs.shape[0], block, LAGS))
        base = base + QUAD * chans
    return held


def solution(mesh):
    placed = (
        P(None, ("group", "chan"), None),
        P(("group", "chan")),
        P(None, ("group", "chan")),
        P(("group", "chan"), None),
    )
    return jax.shard_map(
        body,
        mesh=mesh,
        in_specs=placed,
        out_specs=P(("group", "chan"), None, None),
        check_vma=False,
    )
```

```python
import functools
import math

import jax
import jax.numpy as jnp
import numpy as np
from jax import lax
from jax.experimental import pallas as pl
from jax.experimental.pallas import tpu as pltpu
from jax.sharding import PartitionSpec as P

LAGS = 512
QUAD = 4
CHANS = 8
STEP = 256
VMEM_BYTES = 50 << 20
MASKS = (0, 2, 1, 3)

SMEM = pl.BlockSpec(memory_space=pltpu.SMEM)
ANY = pl.BlockSpec(memory_space=pl.ANY)


def bin_order(bins):
    return np.concatenate([np.arange(2, bins + 1, 2), np.arange(1, bins + 1, 2)])


def make_basis(width, bins):
    rows = np.arange(width // 2, dtype=np.int64)[:, None]
    phase = (rows * bin_order(bins)[None, :] % width) * (2.0 * math.pi / width)
    table = np.stack([np.cos(phase), -np.sin(phase)]).reshape(2, width // 2, bins // STEP, STEP)
    table = table.transpose(2, 1, 0, 3).reshape(bins // STEP, width // 2, 2 * STEP)
    return table.astype(np.float32).astype(jnp.bfloat16)


def make_hann(width):
    hann = 0.5 - 0.5 * np.cos(np.arange(width // 2) * (2.0 * math.pi / width))
    return np.stack([hann, 1.0 - hann]).astype(np.float32)


def make_lagmap(width, bins, lags):
    rows = bin_order(bins)[:, None]
    cols = np.arange(lags, dtype=np.int64)[None, :] - lags // 2 + width
    phase = (rows * cols % width) * (2.0 * math.pi / width)
    scale = 2.0 / math.sqrt(bins)
    table = np.concatenate([scale * np.cos(phase), -scale * np.sin(phase)], 0)
    return table.astype(np.float32).astype(jnp.bfloat16)


def to_quad_peer(value, mask):
    count = lax.axis_size("chan")
    return lax.ppermute(value, "chan", [(s, s ^ mask) for s in range(count)])


def swap_quads(value, odd):
    count = lax.axis_size("chan")
    pairs = []
    for s in range(count):
        quad = s // QUAD
        other = s + QUAD if quad % 2 == odd else s - QUAD
        if 0 <= other < count:
            pairs.append((s, other))
    return lax.ppermute(value, "chan", pairs)


def after(value, *others):
    return lax.optimization_barrier((value,) + others)[0]


def whiten_kernel(chunks, first, core, own, got, own_peer, got_peer, curve, basis, *refs):
    outs = refs[:chunks]
    raw, table, hann, re_s, im_s, amp_s, result, sems, out_sem = refs[chunks:]
    windows, both = raw.shape[1:3]
    half = raw.shape[3] // 2
    steps = basis.shape[0]
    bins = steps * STEP
    copies = [
        pltpu.make_async_copy(own.at[:, pl.ds(first, both)], raw.at[0], sems.at[0]),
        pltpu.make_async_copy(got, raw.at[1], sems.at[1]),
        pltpu.make_async_copy(own_peer.at[:, pl.ds(first, both)], raw.at[2], sems.at[2]),
        pltpu.make_async_copy(got_peer, raw.at[3], sems.at[3]),
        pltpu.make_async_copy(curve, hann, sems.at[4]),
    ]
    tables = [
        pltpu.make_async_copy(basis.at[j], table.at[j], sems.at[QUAD + 1 + j])
        for j in range(steps)
    ]
    for copy in copies + tables:
        copy.start()
    for copy in copies:
        copy.wait()
    low = core[0] == 0
    sums, gaps = [], []
    for c in range(chunks):
        low_at = slice(2 * c * CHANS, (2 * c + 1) * CHANS)
        high_at = slice((2 * c + 1) * CHANS, (2 * c + 2) * CHANS)
        for r in range(QUAD):
            for w in range(windows):
                left = raw[r, w, :, 0:half].astype(jnp.float32)
                right = raw[r, w, :, half:].astype(jnp.float32)
                left = jnp.where(low, left[low_at], left[high_at]) * hann[0:1, :]
                right = jnp.where(low, right[low_at], right[high_at]) * hann[1:2, :]
                sums.append(left + right)
                gaps.append(left - right)
    folded = [jnp.concatenate(x, 0).astype(jnp.bfloat16) for x in (sums, gaps)]
    rows = QUAD * windows * CHANS
    total = jnp.zeros((chunks * rows, 128), jnp.float32)
    for j in range(steps):
        tables[j].wait()
        both_parts = jnp.dot(
            folded[2 * j // steps], table[j], preferred_element_type=jnp.float32
        )
        re, im = both_parts[:, :STEP], both_parts[:, STEP:]
        amp = jnp.sqrt(re * re + im * im)
        at = slice(j * STEP, (j + 1) * STEP)
        re_s[:, at] = re
        im_s[:, at] = im
        amp_s[:, at] = amp
        for i in range(0, STEP, 128):
            total = total + amp[:, i : i + 128]
    level = jnp.sum(total, axis=-1, keepdims=True) * (1.0 / bins) + 1e-06
    for j in range(0, bins, STEP):
        factor = 1.0 / (amp_s[:, j : j + STEP] + level)
        result[:, j : j + STEP] = (re_s[:, j : j + STEP] * factor).astype(jnp.bfloat16)
        result[:, bins + j : bins + j + STEP] = (im_s[:, j : j + STEP] * factor).astype(
            jnp.bfloat16
        )
    writes = [
        pltpu.make_async_copy(result.at[pl.ds(c * rows, rows)], outs[c], out_sem.at[c])
        for c in range(chunks)
    ]
    for write in writes:
        write.start()
    for write in writes:
        write.wait()


def whiten(first, core, own, got, own_peer, got_peer, hann, basis):
    windows, both, width = got.shape
    chunks = both // (2 * CHANS)
    rows = QUAD * windows * CHANS
    total = chunks * rows
    bins = width // 2
    return pl.pallas_call(
        functools.partial(whiten_kernel, chunks, first),
        out_shape=[jax.ShapeDtypeStruct((rows, width), jnp.bfloat16)] * chunks,
        in_specs=[SMEM] + [ANY] * 6,
        out_specs=[ANY] * chunks,
        scratch_shapes=[
            pltpu.VMEM((QUAD, windows, both, width), jnp.bfloat16),
            pltpu.VMEM(basis.shape, jnp.bfloat16),
            pltpu.VMEM(hann.shape, jnp.float32),
            pltpu.VMEM((total, bins), jnp.float32),
            pltpu.VMEM((total, bins), jnp.float32),
            pltpu.VMEM((total, bins), jnp.float32),
            pltpu.VMEM((total, width), jnp.bfloat16),
            pltpu.SemaphoreType.DMA((QUAD + 1 + basis.shape[0],)),
            pltpu.SemaphoreType.DMA((chunks,)),
        ],
        compiler_params=pltpu.CompilerParams(vmem_limit_bytes=VMEM_BYTES),
        cost_estimate=pl.CostEstimate(flops=1024, bytes_accessed=1024, transcendentals=0),
        name="whiten",
    )(core, own, got, own_peer, got_peer, hann, basis)


def cross_kernel(sides, chunk, spot, windows, place, filled, *refs):
    count = len(sides)
    blocks, flags, lagmap = refs[:3], refs[3], refs[4]
    outs = refs[-count - 8 : -8]
    raw, live, near, cross, table, result, sems, out_sems = refs[-8:]
    width = near.shape[-1]
    bins = width // 2
    pairs = place.shape[0] // 2
    copies = [pltpu.make_async_copy(b, raw.at[i], sems.at[i]) for i, b in enumerate(blocks)]
    copies.append(pltpu.make_async_copy(flags.at[chunk], live, sems.at[3]))
    load = pltpu.make_async_copy(lagmap, table, sems.at[4])
    for copy in copies:
        copy.start()
    load.start()
    for i, copy in enumerate(copies):
        copy.wait()
        if i < 3:
            near[pl.ds(i * QUAD, QUAD)] = (
                raw[i].astype(jnp.float32).reshape(QUAD, windows, CHANS, width)
            )

    def one(p):
        a, b = near.at[place[p, 0]], near.at[place[p, 1]]
        live_a, live_b = live.at[place[p, 0]], live.at[place[p, 1]]
        total = live_a[0] * live_b[0]
        for w in range(1, windows):
            total = total + live_a[w] * live_b[w]
        scale = jnp.where(filled[p] > 0, 1.0, 0.0) * (1.0 / jnp.maximum(total, 1.0))
        res, ims = [], []
        for j in range(0, bins, 128):
            re = im = None
            for w in range(windows):
                ra, ia = a[w, :, j : j + 128], a[w, :, bins + j : bins + j + 128]
                rb, ib = b[w, :, j : j + 128], b[w, :, bins + j : bins + j + 128]
                x, y = ra * rb + ia * ib, ra * ib - ia * rb
                re = x if re is None else re + x
                im = y if im is None else im + y
            res.append(re * scale)
            ims.append(im * scale)
        return res + ims

    writes = []
    for n, side in enumerate(sides):
        base = side * pairs

        def two(h, carry):
            p = base + 2 * h
            some = filled[p] + filled[p + 1] > 0

            @pl.when(some)
            def _():
                for j, (u, v) in enumerate(zip(one(p), one(p + 1))):
                    cross[h, :, j * 128 : (j + 1) * 128] = jnp.concatenate([u, v], 0).astype(
                        jnp.bfloat16
                    )

            @pl.when(jnp.logical_not(some))
            def _():
                cross[h] = jnp.zeros(cross.shape[1:], jnp.bfloat16)

            return carry

        lax.fori_loop(0, pairs // 2, two, 0)
        if n == 0:
            load.wait()
        result[n] = jnp.dot(
            cross[...].reshape(pairs * CHANS, width),
            table[...],
            preferred_element_type=jnp.float32,
        ).astype(jnp.bfloat16)
        write = pltpu.make_async_copy(result.at[n], outs[n].at[spot], out_sems.at[n])
        write.start()
        writes.append(write)
    for write in writes:
        write.wait()


def cross_stack(sides, chunk, spot, depth, place, filled, blocks, flags, lagmap, held):
    count = len(sides)
    pairs = place.shape[0] // 2
    rows, width = blocks[0].shape
    windows = flags.shape[2]
    return pl.pallas_call(
        functools.partial(cross_kernel, sides, chunk, spot, windows),
        out_shape=[jax.ShapeDtypeStruct((depth, pairs * CHANS, LAGS), jnp.bfloat16)] * count,
        in_specs=[SMEM, SMEM] + [ANY] * (5 + len(held)),
        out_specs=[ANY] * count,
        input_output_aliases={7 + n: n for n in range(len(held))},
        scratch_shapes=[
            pltpu.VMEM((3, rows, width), jnp.bfloat16),
            pltpu.VMEM(flags.shape[1:], jnp.float32),
            pltpu.VMEM((3 * QUAD, windows, CHANS, width), jnp.float32),
            pltpu.VMEM((pairs * CHANS // 16, 16, width), jnp.bfloat16),
            pltpu.VMEM((width, LAGS), jnp.bfloat16),
            pltpu.VMEM((count, pairs * CHANS, LAGS), jnp.bfloat16),
            pltpu.SemaphoreType.DMA((5,)),
            pltpu.SemaphoreType.DMA((count,)),
        ],
        compiler_params=pltpu.CompilerParams(vmem_limit_bytes=VMEM_BYTES),
        cost_estimate=pl.CostEstimate(flops=1024, bytes_accessed=1024, transcendentals=0),
        name="cross_stack",
    )(place, filled, *blocks, flags, lagmap, *held)


def place_kernel(slot, r0, r1, r2, r3, *refs):
    out = refs[-1]
    for m, r in enumerate((r0, r1, r2, r3)):
        at = pl.multiple_of(slot[m] % 2 * CHANS, CHANS)
        chip = slot[m] // 2
        for p in range(0, out.shape[0], 2):
            wide = r[0, 0, pl.ds(p * CHANS, 2 * CHANS), :].astype(jnp.float32)
            out[p, chip, pl.ds(at, CHANS), :] = wide[:CHANS]
            out[p + 1, chip, pl.ds(at, CHANS), :] = wide[CHANS:]


def place_stacks(first, slot, parts, held, shape):
    extra = [] if held is None else [held]
    step = 8
    depth = parts[0].shape[0]
    parts = [part.reshape(depth, 2, -1, LAGS) for part in parts]
    spot = [
        pl.BlockSpec((1, 1, step * CHANS, LAGS), lambda c, i, *_, k=k: (c, k, i, 0))
        for k in (0, 0, 1, 1)
    ]
    return pl.pallas_call(
        place_kernel,
        out_shape=jax.ShapeDtypeStruct(shape, jnp.float32),
        grid_spec=pltpu.PrefetchScalarGridSpec(
            num_scalar_prefetch=1,
            grid=(depth, shape[0] // step),
            in_specs=spot + [ANY] * len(extra),
            out_specs=pl.BlockSpec(
                (step, 2, 2 * CHANS, LAGS), lambda c, i, *_: (i, 0, first + c, 0)
            ),
        ),
        input_output_aliases={5: 0} if extra else {},
        compiler_params=pltpu.CompilerParams(vmem_limit_bytes=VMEM_BYTES),
        cost_estimate=pl.CostEstimate(flops=1024, bytes_accessed=1024, transcendentals=0),
        name="place_stacks",
    )(slot, *parts, *extra)


def body(records, dead, glitch, pairs):
    windows, block, width = records.shape
    bins = width // 2
    slots = pairs.shape[0]
    half = block // 2
    wide = 2 * CHANS
    chunks = half // wide
    here = lax.axis_index("chan")
    mine = here % QUAD
    quad = here // QUAD
    chip = mine // 2
    core = (mine % 2).reshape(1).astype(jnp.int32)
    basis = jnp.asarray(make_basis(width, bins))
    hann = jnp.asarray(make_hann(width))
    lagmap = jnp.asarray(make_lagmap(width, bins, LAGS))
    live = dead[None, :] * glitch
    live_wire = live.astype(jnp.bfloat16)[..., None]

    def cut(at, count):
        raw = lax.dynamic_slice_in_dim(records, at, count, 1)
        return raw * lax.dynamic_slice_in_dim(live_wire, at, count, 1)

    there = (1 - chip) * half
    notes = jnp.concatenate([live.reshape(-1), pairs.reshape(-1)]).astype(jnp.float32)
    send, at = lax.optimization_barrier((cut(there, wide), chip * half))
    got = [to_quad_peer(send, 2)]
    own, there = lax.optimization_barrier((cut(at, half), there))
    own_peer = to_quad_peer(own, 1)
    notes, there = lax.optimization_barrier((notes, there))
    send, there = lax.optimization_barrier((cut(there + wide, wide), there))
    got.append(to_quad_peer(send, 2))
    notes = jnp.stack([notes, to_quad_peer(notes, 2)])
    got.append(to_quad_peer(cut(there + 2 * wide, half - 2 * wide), 2))
    got_peer = [to_quad_peer(got[0], 1)]
    notes = jnp.concatenate([notes, to_quad_peer(notes, 1)])

    white = []
    for c in range(3):
        if c:
            got_peer.append(to_quad_peer(after(got[c], white[-1]), 1))
        white += whiten(c * wide, core, own, got[c], own_peer, got_peer[c], hann, basis)
    near = [(swap_quads(w, 0), w, swap_quads(w, 1)) for w in white]

    flags = notes[:, : windows * block]
    sent = after(flags, got_peer[1])
    flags = jnp.stack([swap_quads(sent, 0), flags, swap_quads(sent, 1)])
    flags = flags.reshape(3 * QUAD, windows, 2, chunks, 2, CHANS)
    flags = lax.dynamic_index_in_dim(flags, chip, 2, False)
    flags = lax.dynamic_index_in_dim(flags, core[0], 3, False)
    flags = jnp.broadcast_to(
        flags.transpose(2, 0, 1, 3)[..., None], (chunks, 3 * QUAD, windows, CHANS, 128)
    )

    listed = notes[:, windows * block :].astype(jnp.int32).reshape(2, 2, slots, 2)
    listed = listed.swapaxes(0, 1)[::-1].reshape(-1, 2)
    filled = (listed[..., 0] >= 0) & (listed[..., 1] >= 0)
    inside = (listed % QUAD) ^ mine
    side = jnp.where(quad % 2 == 0, 1, -1)
    place = (1 - (listed // QUAD - quad) * side) * QUAD + (inside % 2) * 2 + inside // 2
    place = jnp.where(filled[..., None], jnp.clip(place, 0, 3 * QUAD - 1), 0)
    filled = filled.astype(jnp.int32)
    slot = jnp.stack([mine ^ m for m in MASKS]).astype(jnp.int32)
    shape = (slots, 2, half, LAGS)

    def cross(sides, c, spot, depth, place, held=()):
        return cross_stack(
            sides, c, spot, depth, place, filled, near[c], flags, lagmap, tuple(held)
        )

    def returned(home, away):
        return (home, away, to_quad_peer(home, 1), to_quad_peer(away, 1))

    place = after(place, *white)
    both = cross((0, 1), 0, 0, 2, place)
    away, home = cross((0, 1), 1, 1, 2, place, both)
    parts = returned(home, to_quad_peer(away, 2))
    away, home = cross((0, 1), 2, 0, 1, after(place, home))
    away = to_quad_peer(away, 2)
    held = place_stacks(0, slot, parts, None, shape)
    parts = returned(home, away)
    (away,) = cross((0,), 3, 0, 1, after(place, home, held))
    away = to_quad_peer(away, 2)
    held = place_stacks(2, slot, parts, held, shape)
    (home,) = cross((1,), 3, 0, 1, after(place, held))
    held = place_stacks(3, slot, returned(home, away), held, shape)
    return held.reshape(slots, block, LAGS)


def solution(mesh):
    placed = (
        P(None, ("group", "chan"), None),
        P(("group", "chan")),
        P(None, ("group", "chan")),
        P(("group", "chan"), None),
    )
    return jax.shard_map(
        body,
        mesh=mesh,
        in_specs=placed,
        out_specs=P(("group", "chan"), None, None),
        check_vma=False,
    )
```

```python
import functools
import math

import jax
import jax.numpy as jnp
import numpy as np
from jax import lax
from jax.experimental import pallas as pl
from jax.experimental.pallas import tpu as pltpu
from jax.sharding import PartitionSpec as P

LAGS = 512
QUAD = 4
CHANS = 8
STEP = 256
WHITEN_US, CROSS_US, PLACE_US = 2, 3.2, 1.5
VMEM_BYTES = 50 << 20
MASKS = (0, 2, 1, 3)

SMEM = pl.BlockSpec(memory_space=pltpu.SMEM)
ANY = pl.BlockSpec(memory_space=pl.ANY)


def cost(us):
    return pl.CostEstimate(flops=int(us * 1e9), bytes_accessed=1024, transcendentals=0)


def bin_order(bins):
    return np.concatenate([np.arange(2, bins + 1, 2), np.arange(1, bins + 1, 2)])


def make_basis(width, bins):
    rows = np.arange(width // 2, dtype=np.int64)[:, None]
    phase = (rows * bin_order(bins)[None, :] % width) * (2.0 * math.pi / width)
    table = np.stack([np.cos(phase), -np.sin(phase)]).reshape(2, width // 2, bins // STEP, STEP)
    table = table.transpose(2, 1, 0, 3).reshape(bins // STEP, width // 2, 2 * STEP)
    return table.astype(np.float32).astype(jnp.bfloat16)


def make_hann(width):
    hann = 0.5 - 0.5 * np.cos(np.arange(width // 2) * (2.0 * math.pi / width))
    return np.stack([hann, 1.0 - hann]).astype(np.float32)


def make_lagmap(width, bins, lags):
    rows = bin_order(bins)[:, None]
    cols = np.arange(lags, dtype=np.int64)[None, :] - lags // 2 + width
    phase = (rows * cols % width) * (2.0 * math.pi / width)
    scale = 2.0 / math.sqrt(bins)
    table = np.concatenate([scale * np.cos(phase), -scale * np.sin(phase)], 0)
    return table.astype(np.float32).astype(jnp.bfloat16)


def to_quad_peer(value, mask, name):
    count = lax.axis_size("chan")
    with jax.named_scope(name):
        return lax.ppermute(value, "chan", [(s, s ^ mask) for s in range(count)])


def swap_quads(value, odd, name):
    count = lax.axis_size("chan")
    pairs = []
    for s in range(count):
        quad = s // QUAD
        other = s + QUAD if quad % 2 == odd else s - QUAD
        if 0 <= other < count:
            pairs.append((s, other))
    with jax.named_scope(name):
        return lax.ppermute(value, "chan", pairs)


def after(value, *others):
    return lax.optimization_barrier((value,) + others)[0]


def whiten_kernel(chunks, first, meta, own, got, own_peer, got_peer, curve, basis, *refs):
    outs = refs[:chunks]
    raw, raw_got, table, hann, re_s, im_s, amp_s, result, sems, out_sem = refs[chunks:]
    windows, both = raw.shape[1:3]
    half = raw.shape[3] // 2
    steps = basis.shape[0]
    bins = steps * STEP
    here = pl.ds(pl.multiple_of(meta[1] + first, 16), both)
    copies = [
        pltpu.make_async_copy(own.at[:, here], raw.at[0], sems.at[0]),
        pltpu.make_async_copy(got.at[pl.ds(0, windows * both)], raw_got.at[0], sems.at[1]),
        pltpu.make_async_copy(own_peer.at[:, here], raw.at[1], sems.at[2]),
        pltpu.make_async_copy(got_peer.at[pl.ds(0, windows * both)], raw_got.at[1], sems.at[3]),
        pltpu.make_async_copy(curve, hann, sems.at[4]),
    ]
    tables = [
        pltpu.make_async_copy(basis.at[j], table.at[j], sems.at[QUAD + 1 + j])
        for j in range(steps)
    ]
    for copy in copies + tables:
        copy.start()
    for copy in copies:
        copy.wait()
    low = meta[0] == 0
    sums, gaps = [], []
    for c in range(chunks):
        low_at = slice(2 * c * CHANS, (2 * c + 1) * CHANS)
        high_at = slice((2 * c + 1) * CHANS, (2 * c + 2) * CHANS)
        for r in range(QUAD):
            for w in range(windows):
                if r % 2:
                    whole = raw_got[r // 2, pl.ds(w * both, both), :].astype(jnp.float32)
                else:
                    whole = raw[r // 2, w].astype(jnp.float32)
                left, right = whole[:, :half], whole[:, half:]
                left = jnp.where(low, left[low_at], left[high_at]) * hann[0:1, :]
                right = jnp.where(low, right[low_at], right[high_at]) * hann[1:2, :]
                sums.append(left + right)
                gaps.append(left - right)
    folded = [jnp.concatenate(x, 0).astype(jnp.bfloat16) for x in (sums, gaps)]
    rows = QUAD * windows * CHANS
    total = jnp.zeros((chunks * rows, 128), jnp.float32)
    for j in range(steps):
        tables[j].wait()
        both_parts = jnp.dot(
            folded[2 * j // steps], table[j], preferred_element_type=jnp.float32
        )
        re, im = both_parts[:, :STEP], both_parts[:, STEP:]
        amp = jnp.sqrt(re * re + im * im)
        at = slice(j * STEP, (j + 1) * STEP)
        re_s[:, at] = re
        im_s[:, at] = im
        amp_s[:, at] = amp
        for i in range(0, STEP, 128):
            total = total + amp[:, i : i + 128]
    level = jnp.sum(total, axis=-1, keepdims=True) * (1.0 / bins) + 1e-06
    for j in range(0, bins, STEP):
        factor = 1.0 / (amp_s[:, j : j + STEP] + level)
        result[:, j : j + STEP] = (re_s[:, j : j + STEP] * factor).astype(jnp.bfloat16)
        result[:, bins + j : bins + j + STEP] = (im_s[:, j : j + STEP] * factor).astype(
            jnp.bfloat16
        )
    writes = [
        pltpu.make_async_copy(result.at[pl.ds(c * rows, rows)], outs[c], out_sem.at[c])
        for c in range(chunks)
    ]
    for write in writes:
        write.start()
    for write in writes:
        write.wait()


def whiten(first, chunks, meta, own, got, own_peer, got_peer, hann, basis):
    windows, _, width = own.shape
    both = chunks * 2 * CHANS
    rows = QUAD * windows * CHANS
    total = chunks * rows
    bins = width // 2
    return pl.pallas_call(
        functools.partial(whiten_kernel, chunks, first),
        out_shape=[jax.ShapeDtypeStruct((rows, width), jnp.bfloat16)] * chunks,
        in_specs=[SMEM] + [ANY] * 6,
        out_specs=[ANY] * chunks,
        scratch_shapes=[
            pltpu.VMEM((2, windows, both, width), jnp.bfloat16),
            pltpu.VMEM((2, windows * both, width), jnp.bfloat16),
            pltpu.VMEM(basis.shape, jnp.bfloat16),
            pltpu.VMEM(hann.shape, jnp.float32),
            pltpu.VMEM((total, bins), jnp.float32),
            pltpu.VMEM((total, bins), jnp.float32),
            pltpu.VMEM((total, bins), jnp.float32),
            pltpu.VMEM((total, width), jnp.bfloat16),
            pltpu.SemaphoreType.DMA((QUAD + 1 + basis.shape[0],)),
            pltpu.SemaphoreType.DMA((chunks,)),
        ],
        compiler_params=pltpu.CompilerParams(vmem_limit_bytes=VMEM_BYTES),
        cost_estimate=cost(WHITEN_US * chunks),
        name="whiten",
    )(meta, own, got, own_peer, got_peer, hann, basis)


def cross_kernel(sides, chunk, windows, meta, place, filled, *refs):
    count = len(sides)
    blocks, flags, lagmap = refs[:3], refs[3], refs[4]
    outs = refs[-count - 9 : -9]
    raw, held, live, near, cross, table, result, sems, out_sems = refs[-9:]
    width = near.shape[-1]
    bins = width // 2
    pairs = place.shape[0] // 2
    copies = [pltpu.make_async_copy(b, raw.at[i], sems.at[i]) for i, b in enumerate(blocks)]
    copies.insert(0, pltpu.make_async_copy(flags, held, sems.at[3]))
    load = pltpu.make_async_copy(lagmap, table, sems.at[4])
    for copy in copies:
        copy.start()
    load.start()
    for i, copy in enumerate(copies):
        copy.wait()
        if i == 0:
            shape = (CHANS, held.shape[1])
            first = meta[1] + meta[0] * CHANS + chunk * 2 * CHANS
            pick = lax.broadcasted_iota(jnp.int32, shape, 1) == first + lax.broadcasted_iota(
                jnp.int32, shape, 0
            )
            picked = lax.dot_general(
                jnp.where(pick, 1.0, 0.0).astype(jnp.bfloat16),
                held[...],
                (((1,), (1,)), ((), ())),
                preferred_element_type=jnp.float32,
            )
            for k in range(held.shape[0]):
                live[k // windows, k % windows] = jnp.broadcast_to(
                    picked[:, k : k + 1], (CHANS, 128)
                )
            continue
        wide = raw[i - 1].astype(jnp.float32).reshape(QUAD, windows, CHANS, width)
        for r in range(QUAD):
            for w in range(windows):
                flag = live[(i - 1) * QUAD + r, w][:, 0:1]
                near[(i - 1) * QUAD + r, w] = wide[r, w] * flag

    def one(p):
        a, b = near.at[place[p, 0]], near.at[place[p, 1]]
        live_a, live_b = live.at[place[p, 0]], live.at[place[p, 1]]
        total = live_a[0] * live_b[0]
        for w in range(1, windows):
            total = total + live_a[w] * live_b[w]
        scale = jnp.where(filled[p] > 0, 1.0, 0.0) * (1.0 / jnp.maximum(total, 1.0))
        res, ims = [], []
        for j in range(0, bins, 128):
            re = im = None
            for w in range(windows):
                ra, ia = a[w, :, j : j + 128], a[w, :, bins + j : bins + j + 128]
                rb, ib = b[w, :, j : j + 128], b[w, :, bins + j : bins + j + 128]
                x, y = ra * rb + ia * ib, ra * ib - ia * rb
                re = x if re is None else re + x
                im = y if im is None else im + y
            res.append(re * scale)
            ims.append(im * scale)
        return res + ims

    writes = []
    for n, side in enumerate(sides):
        base = side * pairs

        def two(h, carry):
            p = base + 2 * h
            some = filled[p] + filled[p + 1] > 0

            @pl.when(some)
            def _():
                for j, (u, v) in enumerate(zip(one(p), one(p + 1))):
                    cross[h, :, j * 128 : (j + 1) * 128] = jnp.concatenate([u, v], 0).astype(
                        jnp.bfloat16
                    )

            @pl.when(jnp.logical_not(some))
            def _():
                cross[h] = jnp.zeros(cross.shape[1:], jnp.bfloat16)

            return carry

        lax.fori_loop(0, pairs // 2, two, 0)
        if n == 0:
            load.wait()
        result[n] = jnp.dot(
            cross[...].reshape(pairs * CHANS, width),
            table[...],
            preferred_element_type=jnp.float32,
        ).astype(jnp.bfloat16)
        write = pltpu.make_async_copy(result.at[n], outs[n].at[0], out_sems.at[n])
        write.start()
        writes.append(write)
    for write in writes:
        write.wait()


def cross_stack(sides, chunk, windows, meta, place, filled, blocks, flags, lagmap):
    count = len(sides)
    pairs = place.shape[0] // 2
    rows, width = blocks[0].shape
    return pl.pallas_call(
        functools.partial(cross_kernel, sides, chunk, windows),
        out_shape=[jax.ShapeDtypeStruct((1, pairs * CHANS, LAGS), jnp.bfloat16)] * count,
        in_specs=[SMEM] * 3 + [ANY] * 5,
        out_specs=[ANY] * count,
        scratch_shapes=[
            pltpu.VMEM((3, rows, width), jnp.bfloat16),
            pltpu.VMEM(flags.shape, jnp.bfloat16),
            pltpu.VMEM((3 * QUAD, windows, CHANS, 128), jnp.float32),
            pltpu.VMEM((3 * QUAD, windows, CHANS, width), jnp.float32),
            pltpu.VMEM((pairs * CHANS // 16, 16, width), jnp.bfloat16),
            pltpu.VMEM((width, LAGS), jnp.bfloat16),
            pltpu.VMEM((count, pairs * CHANS, LAGS), jnp.bfloat16),
            pltpu.SemaphoreType.DMA((5,)),
            pltpu.SemaphoreType.DMA((count,)),
        ],
        compiler_params=pltpu.CompilerParams(vmem_limit_bytes=VMEM_BYTES),
        cost_estimate=cost(CROSS_US * count),
        name="cross_stack",
    )(meta, place, filled, *blocks, flags, lagmap)


def place_kernel(slot, r0, r1, r2, r3, *refs):
    out = refs[-1]
    for m, r in enumerate((r0, r1, r2, r3)):
        at = pl.multiple_of(slot[m] % 2 * CHANS, CHANS)
        chip = slot[m] // 2
        for p in range(0, out.shape[0], 2):
            wide = r[0, 0, pl.ds(p * CHANS, 2 * CHANS), :].astype(jnp.float32)
            out[p, chip, pl.ds(at, CHANS), :] = wide[:CHANS]
            out[p + 1, chip, pl.ds(at, CHANS), :] = wide[CHANS:]


def place_stacks(first, slot, parts, held, shape):
    extra = [] if held is None else [held]
    step = 8
    depth = parts[0].shape[0]
    parts = [part.reshape(depth, 2, -1, LAGS) for part in parts]
    spot = [
        pl.BlockSpec((1, 1, step * CHANS, LAGS), lambda c, i, *_, k=k: (c, k, i, 0))
        for k in (0, 0, 1, 1)
    ]
    return pl.pallas_call(
        place_kernel,
        out_shape=jax.ShapeDtypeStruct(shape, jnp.float32),
        grid_spec=pltpu.PrefetchScalarGridSpec(
            num_scalar_prefetch=1,
            grid=(depth, shape[0] // step),
            in_specs=spot + [ANY] * len(extra),
            out_specs=pl.BlockSpec(
                (step, 2, 2 * CHANS, LAGS), lambda c, i, *_: (i, 0, first + c, 0)
            ),
        ),
        input_output_aliases={5: 0} if extra else {},
        compiler_params=pltpu.CompilerParams(vmem_limit_bytes=VMEM_BYTES),
        cost_estimate=cost(PLACE_US * depth),
        name="place_stacks",
    )(slot, *parts, *extra)


def body(records, dead, glitch, pairs):
    windows, block, width = records.shape
    bins = width // 2
    slots = pairs.shape[0]
    half = block // 2
    wide = 2 * CHANS
    chunks = half // wide
    here = lax.axis_index("chan")
    mine = here % QUAD
    quad = here // QUAD
    chip = mine // 2
    meta = jnp.stack([mine % 2, chip * half]).astype(jnp.int32)
    basis = jnp.asarray(make_basis(width, bins))
    hann = jnp.asarray(make_hann(width))
    lagmap = jnp.asarray(make_lagmap(width, bins, LAGS))
    def cut(at, count):
        return lax.dynamic_slice_in_dim(records, at, count, 1).reshape(-1, width)

    there = (1 - chip) * half
    send, there = lax.optimization_barrier((cut(there, wide), there))
    got = [to_quad_peer(send, 2, "Y0_")]
    own_peer = to_quad_peer(records, 1, "CA_")
    live = after((dead[None, :] * glitch).astype(jnp.bfloat16).reshape(-1), send)
    notes = jnp.concatenate([swap_quads(live, 0, "NE_"), live, swap_quads(live, 1, "NO_")])
    notes = jnp.concatenate([notes, pairs.reshape(-1).astype(jnp.bfloat16)])
    size = notes.shape[0]
    page = jnp.pad(notes, (0, 16 * width - size)).reshape(16, width)
    got.append(to_quad_peer(jnp.concatenate([cut(there + wide, wide), page]), 2, "Y1_"))
    got.append(to_quad_peer(cut(there + 2 * wide, half - 2 * wide), 2, "Y2_"))
    white, near, got_peer = [], [], []

    def whiten_next(c, count, *earlier):
        got_peer.append(to_quad_peer(after(got[c], *earlier), 1, f"CB{c}_"))
        for w in whiten(c * wide, count, meta, records, got[c], own_peer, got_peer[c], hann, basis):
            n = len(white)
            near.append((swap_quads(w, 0, f"Z{n}E_"), w, swap_quads(w, 1, f"Z{n}O_")))
            white.append(w)

    whiten_next(0, 1)
    whiten_next(1, 1, white[0])
    notes_peer = to_quad_peer(after(notes, white[1]), 1, "NC_")
    whiten_next(2, chunks - 2, white[1])
    notes = [notes, got[1][-16:].reshape(-1)[:size], notes_peer, got_peer[1][-16:].reshape(-1)[:size]]
    notes = jnp.stack(notes)
    flags = notes[:, : 3 * windows * block].reshape(QUAD, 3, windows, block).swapaxes(0, 1)
    flags = flags.reshape(-1, block)

    listed = notes[:, 3 * windows * block :].astype(jnp.int32).reshape(2, 2, slots, 2)
    listed = listed.swapaxes(0, 1)[::-1].reshape(-1, 2)
    filled = (listed[..., 0] >= 0) & (listed[..., 1] >= 0)
    inside = (listed % QUAD) ^ mine
    side = jnp.where(quad % 2 == 0, 1, -1)
    place = (1 - (listed // QUAD - quad) * side) * QUAD + (inside % 2) * 2 + inside // 2
    place = jnp.where(filled[..., None], jnp.clip(place, 0, 3 * QUAD - 1), 0)
    filled = filled.astype(jnp.int32)
    slot = jnp.stack([mine ^ m for m in MASKS]).astype(jnp.int32)
    shape = (slots, 2, half, LAGS)

    def cross(sides, c, place):
        return cross_stack(sides, c, windows, meta, place, filled, near[c], flags, lagmap)

    def returned(home, away, name):
        return (
            home,
            away,
            to_quad_peer(home, 1, "H" + name),
            to_quad_peer(away, 1, "F" + name),
        )

    held, sent = None, None
    place = after(place, *white)
    for c in range(chunks - 1):
        away, home = cross((0, 1), c, place)
        if sent:
            held = place_stacks(c - 1, slot, returned(*after(sent, home), str(c - 1) + "_"), held, shape)
        place = after(place, home if held is None else held)
        sent = (home, to_quad_peer(away, 2, f"R{c}_"))
    c = chunks - 1
    (away,) = cross((0,), c, place)
    held = place_stacks(c - 1, slot, returned(*after(sent, away), str(c - 1) + "_"), held, shape)
    away = to_quad_peer(away, 2, f"R{c}_")
    (home,) = cross((1,), c, after(place, held))
    held = place_stacks(c, slot, returned(home, away, str(c) + "_"), held, shape)
    return held.reshape(slots, block, LAGS)


def solution(mesh):
    placed = (
        P(None, ("group", "chan"), None),
        P(("group", "chan")),
        P(None, ("group", "chan")),
        P(("group", "chan"), None),
    )
    return jax.shard_map(
        body,
        mesh=mesh,
        in_specs=placed,
        out_specs=P(("group", "chan"), None, None),
        check_vma=False,
    )
```

```python
import functools
import math

import jax
import jax.numpy as jnp
import numpy as np
from jax import lax
from jax.experimental import pallas as pl
from jax.experimental.pallas import tpu as pltpu
from jax.sharding import PartitionSpec as P

LAGS = 512
QUAD = 4
CHANS = 8
STEP = 256
WHITEN_US, CROSS_US, PLACE_US = 2, 3.2, 1.5
VMEM_BYTES = 50 << 20
MASKS = (0, 2, 1, 3)

SMEM = pl.BlockSpec(memory_space=pltpu.SMEM)
ANY = pl.BlockSpec(memory_space=pl.ANY)


def cost(us):
    return pl.CostEstimate(flops=int(us * 1e9), bytes_accessed=1024, transcendentals=0)


def bin_order(bins):
    return np.concatenate([np.arange(2, bins + 1, 2), np.arange(1, bins + 1, 2)])


def make_basis(width, bins):
    rows = np.arange(width // 2, dtype=np.int64)[:, None]
    phase = (rows * bin_order(bins)[None, :] % width) * (2.0 * math.pi / width)
    table = np.stack([np.cos(phase), -np.sin(phase)]).reshape(2, width // 2, bins // STEP, STEP)
    table = table.transpose(2, 1, 0, 3).reshape(bins // STEP, width // 2, 2 * STEP)
    return table.astype(np.float32).astype(jnp.bfloat16)


def make_hann(width):
    hann = 0.5 - 0.5 * np.cos(np.arange(width // 2) * (2.0 * math.pi / width))
    return np.stack([hann, 1.0 - hann]).astype(np.float32)


def make_lagmap(width, bins, lags):
    rows = bin_order(bins)[:, None]
    cols = np.arange(lags, dtype=np.int64)[None, :] - lags // 2 + width
    phase = (rows * cols % width) * (2.0 * math.pi / width)
    scale = 2.0 / math.sqrt(bins)
    table = np.concatenate([scale * np.cos(phase), -scale * np.sin(phase)], 0)
    return table.astype(np.float32).astype(jnp.bfloat16)


def to_quad_peer(value, mask, name):
    count = lax.axis_size("chan")
    with jax.named_scope(name):
        return lax.ppermute(value, "chan", [(s, s ^ mask) for s in range(count)])


def swap_quads(value, odd, name):
    count = lax.axis_size("chan")
    pairs = []
    for s in range(count):
        quad = s // QUAD
        other = s + QUAD if quad % 2 == odd else s - QUAD
        if 0 <= other < count:
            pairs.append((s, other))
    with jax.named_scope(name):
        return lax.ppermute(value, "chan", pairs)


def after(value, *others):
    return lax.optimization_barrier((value,) + others)[0]


def whiten_kernel(chunks, first, meta, own, got, own_peer, got_peer, curve, basis, *refs):
    outs = refs[:chunks]
    raw, raw_got, table, hann, re_s, im_s, amp_s, result, sems, out_sem = refs[chunks:]
    windows, both = raw.shape[1:3]
    half = raw.shape[3] // 2
    steps = basis.shape[0]
    bins = steps * STEP
    part = both // 2
    here = pl.ds(pl.multiple_of(meta[1] + first, 16), both)
    copies = [
        pltpu.make_async_copy(own.at[:, here], raw.at[0], sems.at[0]),
        pltpu.make_async_copy(got.at[pl.ds(0, windows * part)], raw_got.at[0], sems.at[1]),
        pltpu.make_async_copy(own_peer.at[:, here], raw.at[1], sems.at[2]),
        pltpu.make_async_copy(got_peer.at[pl.ds(0, windows * part)], raw_got.at[1], sems.at[3]),
        pltpu.make_async_copy(curve, hann, sems.at[4]),
    ]
    tables = [
        pltpu.make_async_copy(basis.at[j], table.at[j], sems.at[QUAD + 1 + j])
        for j in range(steps)
    ]
    for copy in copies + tables:
        copy.start()
    for copy in copies:
        copy.wait()
    low = meta[0] == 0
    sums, gaps = [], []
    wide = [x.astype(jnp.float32) for x in (raw_got[0], raw_got[1])]
    for c in range(chunks):
        for r in range(QUAD):
            for w in range(windows):
                if r % 2:
                    at = (w * chunks + c) * CHANS
                    rows = wide[r // 2][at : at + CHANS]
                else:
                    rows = raw[r // 2, w].astype(jnp.float32)
                    at = 2 * c * CHANS
                    rows = jnp.where(low, rows[at : at + CHANS], rows[at + CHANS : at + 2 * CHANS])
                left = rows[:, :half] * hann[0:1, :]
                right = rows[:, half:] * hann[1:2, :]
                sums.append(left + right)
                gaps.append(left - right)
    folded = [jnp.concatenate(x, 0).astype(jnp.bfloat16) for x in (sums, gaps)]
    rows = QUAD * windows * CHANS
    total = jnp.zeros((chunks * rows, 128), jnp.float32)
    for j in range(steps):
        tables[j].wait()
        both_parts = jnp.dot(
            folded[2 * j // steps], table[j], preferred_element_type=jnp.float32
        )
        re, im = both_parts[:, :STEP], both_parts[:, STEP:]
        amp = jnp.sqrt(re * re + im * im)
        at = slice(j * STEP, (j + 1) * STEP)
        re_s[:, at] = re
        im_s[:, at] = im
        amp_s[:, at] = amp
        for i in range(0, STEP, 128):
            total = total + amp[:, i : i + 128]
    level = jnp.sum(total, axis=-1, keepdims=True) * (1.0 / bins) + 1e-06
    for j in range(0, bins, STEP):
        factor = 1.0 / (amp_s[:, j : j + STEP] + level)
        result[:, j : j + STEP] = (re_s[:, j : j + STEP] * factor).astype(jnp.bfloat16)
        result[:, bins + j : bins + j + STEP] = (im_s[:, j : j + STEP] * factor).astype(
            jnp.bfloat16
        )
    writes = [
        pltpu.make_async_copy(result.at[pl.ds(c * rows, rows)], outs[c], out_sem.at[c])
        for c in range(chunks)
    ]
    for write in writes:
        write.start()
    for write in writes:
        write.wait()


def whiten(first, chunks, meta, own, got, own_peer, got_peer, hann, basis):
    windows, _, width = own.shape
    both = chunks * 2 * CHANS
    rows = QUAD * windows * CHANS
    total = chunks * rows
    bins = width // 2
    return pl.pallas_call(
        functools.partial(whiten_kernel, chunks, first),
        out_shape=[jax.ShapeDtypeStruct((rows, width), jnp.bfloat16)] * chunks,
        in_specs=[SMEM] + [ANY] * 6,
        out_specs=[ANY] * chunks,
        scratch_shapes=[
            pltpu.VMEM((2, windows, both, width), jnp.bfloat16),
            pltpu.VMEM((2, windows * both // 2, width), jnp.bfloat16),
            pltpu.VMEM(basis.shape, jnp.bfloat16),
            pltpu.VMEM(hann.shape, jnp.float32),
            pltpu.VMEM((total, bins), jnp.float32),
            pltpu.VMEM((total, bins), jnp.float32),
            pltpu.VMEM((total, bins), jnp.float32),
            pltpu.VMEM((total, width), jnp.bfloat16),
            pltpu.SemaphoreType.DMA((QUAD + 1 + basis.shape[0],)),
            pltpu.SemaphoreType.DMA((chunks,)),
        ],
        compiler_params=pltpu.CompilerParams(vmem_limit_bytes=VMEM_BYTES),
        cost_estimate=cost(WHITEN_US * chunks),
        name="whiten",
    )(meta, own, got, own_peer, got_peer, hann, basis)


def cross_kernel(sides, chunk, windows, meta, place, filled, *refs):
    count = len(sides)
    blocks, flags, lagmap = refs[:3], refs[3], refs[4]
    outs = refs[-count - 9 : -9]
    raw, held, live, near, cross, table, result, sems, out_sems = refs[-9:]
    width = near.shape[-1]
    bins = width // 2
    pairs = place.shape[0] // 2
    copies = [pltpu.make_async_copy(b, raw.at[i], sems.at[i]) for i, b in enumerate(blocks)]
    copies.insert(0, pltpu.make_async_copy(flags, held, sems.at[3]))
    load = pltpu.make_async_copy(lagmap, table, sems.at[4])
    for copy in copies:
        copy.start()
    load.start()
    for i, copy in enumerate(copies):
        copy.wait()
        if i == 0:
            shape = (CHANS, held.shape[1])
            first = meta[1] + meta[0] * CHANS + chunk * 2 * CHANS
            pick = lax.broadcasted_iota(jnp.int32, shape, 1) == first + lax.broadcasted_iota(
                jnp.int32, shape, 0
            )
            picked = lax.dot_general(
                jnp.where(pick, 1.0, 0.0).astype(jnp.bfloat16),
                held[...],
                (((1,), (1,)), ((), ())),
                preferred_element_type=jnp.float32,
            )
            for k in range(held.shape[0]):
                live[k // windows, k % windows] = jnp.broadcast_to(
                    picked[:, k : k + 1], (CHANS, 128)
                )
            continue
        wide = raw[i - 1].astype(jnp.float32).reshape(QUAD, windows, CHANS, width)
        for r in range(QUAD):
            for w in range(windows):
                flag = live[(i - 1) * QUAD + r, w][:, 0:1]
                near[(i - 1) * QUAD + r, w] = wide[r, w] * flag

    def one(p):
        a, b = near.at[place[p, 0]], near.at[place[p, 1]]
        live_a, live_b = live.at[place[p, 0]], live.at[place[p, 1]]
        total = live_a[0] * live_b[0]
        for w in range(1, windows):
            total = total + live_a[w] * live_b[w]
        scale = jnp.where(filled[p] > 0, 1.0, 0.0) * (1.0 / jnp.maximum(total, 1.0))
        res, ims = [], []
        for j in range(0, bins, 128):
            re = im = None
            for w in range(windows):
                ra, ia = a[w, :, j : j + 128], a[w, :, bins + j : bins + j + 128]
                rb, ib = b[w, :, j : j + 128], b[w, :, bins + j : bins + j + 128]
                x, y = ra * rb + ia * ib, ra * ib - ia * rb
                re = x if re is None else re + x
                im = y if im is None else im + y
            res.append(re * scale)
            ims.append(im * scale)
        return res + ims

    writes = []
    for n, side in enumerate(sides):
        base = side * pairs

        def two(h, carry):
            p = base + 2 * h
            some = filled[p] + filled[p + 1] > 0

            @pl.when(some)
            def _():
                for j, (u, v) in enumerate(zip(one(p), one(p + 1))):
                    cross[h, :, j * 128 : (j + 1) * 128] = jnp.concatenate([u, v], 0).astype(
                        jnp.bfloat16
                    )

            @pl.when(jnp.logical_not(some))
            def _():
                cross[h] = jnp.zeros(cross.shape[1:], jnp.bfloat16)

            return carry

        lax.fori_loop(0, pairs // 2, two, 0)
        if n == 0:
            load.wait()
        result[n] = jnp.dot(
            cross[...].reshape(pairs * CHANS, width),
            table[...],
            preferred_element_type=jnp.float32,
        ).astype(jnp.bfloat16)
        write = pltpu.make_async_copy(result.at[n], outs[n].at[0], out_sems.at[n])
        write.start()
        writes.append(write)
    for write in writes:
        write.wait()


def cross_stack(sides, chunk, windows, meta, place, filled, blocks, flags, lagmap):
    count = len(sides)
    pairs = place.shape[0] // 2
    rows, width = blocks[0].shape
    return pl.pallas_call(
        functools.partial(cross_kernel, sides, chunk, windows),
        out_shape=[jax.ShapeDtypeStruct((1, pairs * CHANS, LAGS), jnp.bfloat16)] * count,
        in_specs=[SMEM] * 3 + [ANY] * 5,
        out_specs=[ANY] * count,
        scratch_shapes=[
            pltpu.VMEM((3, rows, width), jnp.bfloat16),
            pltpu.VMEM(flags.shape, jnp.bfloat16),
            pltpu.VMEM((3 * QUAD, windows, CHANS, 128), jnp.float32),
            pltpu.VMEM((3 * QUAD, windows, CHANS, width), jnp.float32),
            pltpu.VMEM((pairs * CHANS // 16, 16, width), jnp.bfloat16),
            pltpu.VMEM((width, LAGS), jnp.bfloat16),
            pltpu.VMEM((count, pairs * CHANS, LAGS), jnp.bfloat16),
            pltpu.SemaphoreType.DMA((5,)),
            pltpu.SemaphoreType.DMA((count,)),
        ],
        compiler_params=pltpu.CompilerParams(vmem_limit_bytes=VMEM_BYTES),
        cost_estimate=cost(CROSS_US * count),
        name="cross_stack",
    )(meta, place, filled, *blocks, flags, lagmap)


def place_kernel(slot, r0, r1, r2, r3, *refs):
    out = refs[-1]
    for m, r in enumerate((r0, r1, r2, r3)):
        at = pl.multiple_of(slot[m] % 2 * CHANS, CHANS)
        chip = slot[m] // 2
        for p in range(0, out.shape[0], 2):
            wide = r[0, 0, pl.ds(p * CHANS, 2 * CHANS), :].astype(jnp.float32)
            out[p, chip, pl.ds(at, CHANS), :] = wide[:CHANS]
            out[p + 1, chip, pl.ds(at, CHANS), :] = wide[CHANS:]


def place_stacks(first, slot, parts, held, shape):
    extra = [] if held is None else [held]
    step = 8
    depth = parts[0].shape[0]
    parts = [part.reshape(depth, 2, -1, LAGS) for part in parts]
    spot = [
        pl.BlockSpec((1, 1, step * CHANS, LAGS), lambda c, i, *_, k=k: (c, k, i, 0))
        for k in (0, 0, 1, 1)
    ]
    return pl.pallas_call(
        place_kernel,
        out_shape=jax.ShapeDtypeStruct(shape, jnp.float32),
        grid_spec=pltpu.PrefetchScalarGridSpec(
            num_scalar_prefetch=1,
            grid=(depth, shape[0] // step),
            in_specs=spot + [ANY] * len(extra),
            out_specs=pl.BlockSpec(
                (step, 2, 2 * CHANS, LAGS), lambda c, i, *_: (i, 0, first + c, 0)
            ),
        ),
        input_output_aliases={5: 0} if extra else {},
        compiler_params=pltpu.CompilerParams(vmem_limit_bytes=VMEM_BYTES),
        cost_estimate=cost(PLACE_US * depth),
        name="place_stacks",
    )(slot, *parts, *extra)


def body(records, dead, glitch, pairs):
    windows, block, width = records.shape
    bins = width // 2
    slots = pairs.shape[0]
    half = block // 2
    wide = 2 * CHANS
    chunks = half // wide
    here = lax.axis_index("chan")
    mine = here % QUAD
    quad = here // QUAD
    chip = mine // 2
    meta = jnp.stack([mine % 2, chip * half]).astype(jnp.int32)
    basis = jnp.asarray(make_basis(width, bins))
    hann = jnp.asarray(make_hann(width))
    lagmap = jnp.asarray(make_lagmap(width, bins, LAGS))
    core = mine % 2
    split = records.reshape(windows, 2, chunks, 2, CHANS, width)

    def cut(c, count, core):
        start = (0, 1 - chip, c, core, 0, 0)
        sizes = (windows, 1, count, 1, CHANS, width)
        return lax.dynamic_slice(split, start, sizes).reshape(-1, width)

    def exchange(c, count, core, *pages):
        near_core = jnp.concatenate([cut(c, count, core), *pages])
        far_core = jnp.concatenate([cut(c, count, 1 - core), *pages])
        near_core, far_core = lax.optimization_barrier((near_core, far_core))
        n = len(got)
        got.append(
            (to_quad_peer(near_core, 2, f"Y{n}A_"), to_quad_peer(far_core, 3, f"Y{n}B_"))
        )
        return near_core

    got = []
    sent = exchange(0, 1, core)
    core = after(core, sent)
    own_peer = to_quad_peer(records, 1, "CA_")
    live = after((dead[None, :] * glitch).astype(jnp.bfloat16).reshape(-1), sent)
    notes = jnp.concatenate([swap_quads(live, 0, "NE_"), live, swap_quads(live, 1, "NO_")])
    notes = jnp.concatenate([notes, pairs.reshape(-1).astype(jnp.bfloat16)])
    size = notes.shape[0]
    page = jnp.pad(notes, (0, 16 * width - size)).reshape(16, width)
    exchange(1, 1, core, page)
    white, near = [], []

    def whiten_next(c, count, *earlier):
        mate = after(meta, *earlier)
        for w in whiten(c * wide, count, mate, records, got[c][0], own_peer, got[c][1], hann, basis):
            n = len(white)
            near.append((swap_quads(w, 0, f"Z{n}E_"), w, swap_quads(w, 1, f"Z{n}O_")))
            white.append(w)

    whiten_next(0, 1)
    exchange(2, chunks - 2, after(core, white[0]))
    notes_peer = to_quad_peer(after(notes, white[0]), 1, "NC_")
    whiten_next(1, 1, notes_peer)
    whiten_next(2, chunks - 2, white[1])
    pages = [after(part, white[1])[-16:].reshape(-1)[:size] for part in got[1]]
    notes = jnp.stack([notes, pages[0], notes_peer, pages[1]])
    flags = notes[:, : 3 * windows * block].reshape(QUAD, 3, windows, block).swapaxes(0, 1)
    flags = flags.reshape(-1, block)

    listed = notes[:, 3 * windows * block :].astype(jnp.int32).reshape(2, 2, slots, 2)
    listed = listed.swapaxes(0, 1)[::-1].reshape(-1, 2)
    filled = (listed[..., 0] >= 0) & (listed[..., 1] >= 0)
    inside = (listed % QUAD) ^ mine
    side = jnp.where(quad % 2 == 0, 1, -1)
    place = (1 - (listed // QUAD - quad) * side) * QUAD + (inside % 2) * 2 + inside // 2
    place = jnp.where(filled[..., None], jnp.clip(place, 0, 3 * QUAD - 1), 0)
    filled = filled.astype(jnp.int32)
    slot = jnp.stack([mine ^ m for m in MASKS]).astype(jnp.int32)
    shape = (slots, 2, half, LAGS)

    def cross(sides, c, place):
        return cross_stack(sides, c, windows, meta, place, filled, near[c], flags, lagmap)

    def returned(home, away, name):
        return (
            home,
            away,
            to_quad_peer(home, 1, "H" + name),
            to_quad_peer(away, 1, "F" + name),
        )

    held, sent = None, None
    place = after(place, *white)
    for c in range(chunks - 1):
        away, home = cross((0, 1), c, place)
        if sent:
            held = place_stacks(c - 1, slot, returned(*after(sent, home), str(c - 1) + "_"), held, shape)
        place = after(place, home if held is None else held)
        sent = (home, to_quad_peer(away, 2, f"R{c}_"))
    c = chunks - 1
    (away,) = cross((0,), c, place)
    held = place_stacks(c - 1, slot, returned(*after(sent, away), str(c - 1) + "_"), held, shape)
    away = to_quad_peer(away, 2, f"R{c}_")
    (home,) = cross((1,), c, after(place, held))
    held = place_stacks(c, slot, returned(home, away, str(c) + "_"), held, shape)
    return held.reshape(slots, block, LAGS)


def solution(mesh):
    placed = (
        P(None, ("group", "chan"), None),
        P(("group", "chan")),
        P(None, ("group", "chan")),
        P(("group", "chan"), None),
    )
    return jax.shard_map(
        body,
        mesh=mesh,
        in_specs=placed,
        out_specs=P(("group", "chan"), None, None),
        check_vma=False,
    )
```

```python
import functools
import math

import jax
import jax.numpy as jnp
import numpy as np
from jax import lax
from jax.experimental import pallas as pl
from jax.experimental.pallas import tpu as pltpu
from jax.sharding import PartitionSpec as P

LAGS = 512
QUAD = 4
CHANS = 8
STEP = 256
WHITEN_US, CROSS_US, PLACE_US = 2, 3.2, 1.5
VMEM_BYTES = 50 << 20
MASKS = (0, 2, 1, 3)

SMEM = pl.BlockSpec(memory_space=pltpu.SMEM)
ANY = pl.BlockSpec(memory_space=pl.ANY)


def cost(us):
    return pl.CostEstimate(flops=int(us * 1e9), bytes_accessed=1024, transcendentals=0)


def bin_order(bins):
    return np.concatenate([np.arange(2, bins + 1, 2), np.arange(1, bins + 1, 2)])


def make_basis(width, bins):
    rows = np.arange(width // 2, dtype=np.int64)[:, None]
    phase = (rows * bin_order(bins)[None, :] % width) * (2.0 * math.pi / width)
    table = np.stack([np.cos(phase), -np.sin(phase)]).reshape(2, width // 2, bins // STEP, STEP)
    table = table.transpose(2, 1, 0, 3).reshape(bins // STEP, width // 2, 2 * STEP)
    return table.astype(np.float32).astype(jnp.bfloat16)


def make_hann(width):
    hann = 0.5 - 0.5 * np.cos(np.arange(width // 2) * (2.0 * math.pi / width))
    return np.stack([hann, 1.0 - hann]).astype(np.float32)


def make_lagmap(width, bins, lags):
    rows = bin_order(bins)[:, None]
    cols = np.arange(lags, dtype=np.int64)[None, :] - lags // 2 + width
    phase = (rows * cols % width) * (2.0 * math.pi / width)
    scale = 2.0 / math.sqrt(bins)
    table = np.concatenate([scale * np.cos(phase), -scale * np.sin(phase)], 0)
    return table.astype(np.float32).astype(jnp.bfloat16)


def to_quad_peer(value, mask, name):
    count = lax.axis_size("chan")
    with jax.named_scope(name):
        return lax.ppermute(value, "chan", [(s, s ^ mask) for s in range(count)])


def swap_quads(value, odd, name):
    count = lax.axis_size("chan")
    pairs = []
    for s in range(count):
        quad = s // QUAD
        other = s + QUAD if quad % 2 == odd else s - QUAD
        if 0 <= other < count:
            pairs.append((s, other))
    with jax.named_scope(name):
        return lax.ppermute(value, "chan", pairs)


def after(value, *others):
    return lax.optimization_barrier((value,) + others)[0]


def whiten_kernel(chunks, first, meta, own, got, own_peer, got_peer, curve, basis, *refs):
    outs = refs[:chunks]
    raw, raw_got, table, hann, re_s, im_s, amp_s, result, sems, out_sem = refs[chunks:]
    windows, both = raw.shape[1:3]
    half = raw.shape[3] // 2
    steps = basis.shape[0]
    bins = steps * STEP
    part = both // 2
    here = pl.ds(pl.multiple_of(meta[1] + first, 16), both)
    copies = [
        pltpu.make_async_copy(own.at[:, here], raw.at[0], sems.at[0]),
        pltpu.make_async_copy(got.at[pl.ds(0, windows * part)], raw_got.at[0], sems.at[1]),
        pltpu.make_async_copy(own_peer.at[:, here], raw.at[1], sems.at[2]),
        pltpu.make_async_copy(got_peer.at[pl.ds(0, windows * part)], raw_got.at[1], sems.at[3]),
        pltpu.make_async_copy(curve, hann, sems.at[4]),
    ]
    tables = [
        pltpu.make_async_copy(basis.at[j], table.at[j], sems.at[QUAD + 1 + j])
        for j in range(steps)
    ]
    for copy in copies + tables:
        copy.start()
    for copy in copies:
        copy.wait()
    low = meta[0] == 0
    sums, gaps = [], []
    wide = [x.astype(jnp.float32) for x in (raw_got[0], raw_got[1])]
    for c in range(chunks):
        for r in range(QUAD):
            for w in range(windows):
                if r % 2:
                    at = (w * chunks + c) * CHANS
                    rows = wide[r // 2][at : at + CHANS]
                else:
                    rows = raw[r // 2, w].astype(jnp.float32)
                    at = 2 * c * CHANS
                    rows = jnp.where(low, rows[at : at + CHANS], rows[at + CHANS : at + 2 * CHANS])
                left = rows[:, :half] * hann[0:1, :]
                right = rows[:, half:] * hann[1:2, :]
                sums.append(left + right)
                gaps.append(left - right)
    folded = [jnp.concatenate(x, 0).astype(jnp.bfloat16) for x in (sums, gaps)]
    rows = QUAD * windows * CHANS
    total = jnp.zeros((chunks * rows, 128), jnp.float32)
    for j in range(steps):
        tables[j].wait()
        both_parts = jnp.dot(
            folded[2 * j // steps], table[j], preferred_element_type=jnp.float32
        )
        re, im = both_parts[:, :STEP], both_parts[:, STEP:]
        amp = jnp.sqrt(re * re + im * im)
        at = slice(j * STEP, (j + 1) * STEP)
        re_s[:, at] = re
        im_s[:, at] = im
        amp_s[:, at] = amp
        for i in range(0, STEP, 128):
            total = total + amp[:, i : i + 128]
    level = jnp.sum(total, axis=-1, keepdims=True) * (1.0 / bins) + 1e-06
    for j in range(0, bins, STEP):
        factor = 1.0 / (amp_s[:, j : j + STEP] + level)
        result[:, j : j + STEP] = (re_s[:, j : j + STEP] * factor).astype(jnp.bfloat16)
        result[:, bins + j : bins + j + STEP] = (im_s[:, j : j + STEP] * factor).astype(
            jnp.bfloat16
        )
    writes = [
        pltpu.make_async_copy(result.at[pl.ds(c * rows, rows)], outs[c], out_sem.at[c])
        for c in range(chunks)
    ]
    for write in writes:
        write.start()
    for write in writes:
        write.wait()


def whiten(first, chunks, meta, own, got, own_peer, got_peer, hann, basis):
    windows, _, width = own.shape
    both = chunks * 2 * CHANS
    rows = QUAD * windows * CHANS
    total = chunks * rows
    bins = width // 2
    return pl.pallas_call(
        functools.partial(whiten_kernel, chunks, first),
        out_shape=[jax.ShapeDtypeStruct((rows, width), jnp.bfloat16)] * chunks,
        in_specs=[SMEM] + [ANY] * 6,
        out_specs=[ANY] * chunks,
        scratch_shapes=[
            pltpu.VMEM((2, windows, both, width), jnp.bfloat16),
            pltpu.VMEM((2, windows * both // 2, width), jnp.bfloat16),
            pltpu.VMEM(basis.shape, jnp.bfloat16),
            pltpu.VMEM(hann.shape, jnp.float32),
            pltpu.VMEM((total, bins), jnp.float32),
            pltpu.VMEM((total, bins), jnp.float32),
            pltpu.VMEM((total, bins), jnp.float32),
            pltpu.VMEM((total, width), jnp.bfloat16),
            pltpu.SemaphoreType.DMA((QUAD + 1 + basis.shape[0],)),
            pltpu.SemaphoreType.DMA((chunks,)),
        ],
        compiler_params=pltpu.CompilerParams(vmem_limit_bytes=VMEM_BYTES),
        cost_estimate=cost(WHITEN_US * chunks),
        name="whiten",
    )(meta, own, got, own_peer, got_peer, hann, basis)


def cross_kernel(sides, chunk, windows, meta, place, filled, *refs):
    count = len(sides)
    blocks, flags, lagmap = refs[:3], refs[3], refs[4]
    outs = refs[-count - 10 : -10]
    raw, held, live, near, mixed, cross, table, result, sems, out_sems = refs[-10:]
    width = near.shape[-1]
    bins = width // 2
    pairs = place.shape[0] // 2
    copies = [pltpu.make_async_copy(b, raw.at[i], sems.at[i]) for i, b in enumerate(blocks)]
    copies.insert(0, pltpu.make_async_copy(flags, held, sems.at[3]))
    load = pltpu.make_async_copy(lagmap, table, sems.at[4])
    for copy in copies:
        copy.start()
    load.start()
    for i, copy in enumerate(copies):
        copy.wait()
        if i == 0:
            shape = (CHANS, held.shape[1])
            first = meta[1] + meta[0] * CHANS + chunk * 2 * CHANS
            pick = lax.broadcasted_iota(jnp.int32, shape, 1) == first + lax.broadcasted_iota(
                jnp.int32, shape, 0
            )
            picked = lax.dot_general(
                jnp.where(pick, 1.0, 0.0).astype(jnp.bfloat16),
                held[...],
                (((1,), (1,)), ((), ())),
                preferred_element_type=jnp.float32,
            )
            for k in range(held.shape[0]):
                live[k // windows, k % windows] = jnp.broadcast_to(
                    picked[:, k : k + 1], (CHANS, 128)
                )
            continue
        wide = raw[i - 1].astype(jnp.float32).reshape(QUAD, windows, CHANS, width)
        for r in range(QUAD):
            for w in range(windows):
                flag = live[(i - 1) * QUAD + r, w][:, 0:1]
                value = wide[r, w] * flag
                near[(i - 1) * QUAD + r, w] = value
                re, im = value[:, :bins], value[:, bins:]
                mixed[(i - 1) * QUAD + r, w, :, :bins] = re + im
                mixed[(i - 1) * QUAD + r, w, :, bins:] = re - im

    def one(p):
        a, b = near.at[place[p, 0]], near.at[place[p, 1]]
        mixed_a, mixed_b = mixed.at[place[p, 0]], mixed.at[place[p, 1]]
        live_a, live_b = live.at[place[p, 0]], live.at[place[p, 1]]
        total = live_a[0] * live_b[0]
        for w in range(1, windows):
            total = total + live_a[w] * live_b[w]
        scale = jnp.where(filled[p] > 0, 1.0, 0.0) * (1.0 / jnp.maximum(total, 1.0))
        res, ims = [], []
        for j in range(0, bins, 128):
            here, there = slice(j, j + 128), slice(bins + j, bins + j + 128)
            first = second = third = None
            for w in range(windows):
                x = a[w, :, here] * b[w, :, here]
                y = a[w, :, there] * b[w, :, there]
                z = mixed_a[w, :, here] * mixed_b[w, :, there]
                first = x if first is None else first + x
                second = y if second is None else second + y
                third = z if third is None else third + z
            re, im = first + second, first - second - third
            res.append(re * scale)
            ims.append(im * scale)
        return res + ims

    writes = []
    for n, side in enumerate(sides):
        base = side * pairs

        def two(h, carry):
            p = base + 2 * h
            some = filled[p] + filled[p + 1] > 0

            @pl.when(some)
            def _():
                for j, (u, v) in enumerate(zip(one(p), one(p + 1))):
                    cross[h, :, j * 128 : (j + 1) * 128] = jnp.concatenate([u, v], 0).astype(
                        jnp.bfloat16
                    )

            @pl.when(jnp.logical_not(some))
            def _():
                cross[h] = jnp.zeros(cross.shape[1:], jnp.bfloat16)

            return carry

        lax.fori_loop(0, pairs // 2, two, 0)
        if n == 0:
            load.wait()
        result[n] = jnp.dot(
            cross[...].reshape(pairs * CHANS, width),
            table[...],
            preferred_element_type=jnp.float32,
        ).astype(jnp.bfloat16)
        write = pltpu.make_async_copy(result.at[n], outs[n].at[0], out_sems.at[n])
        write.start()
        writes.append(write)
    for write in writes:
        write.wait()


def cross_stack(sides, chunk, windows, meta, place, filled, blocks, flags, lagmap):
    count = len(sides)
    pairs = place.shape[0] // 2
    rows, width = blocks[0].shape
    return pl.pallas_call(
        functools.partial(cross_kernel, sides, chunk, windows),
        out_shape=[jax.ShapeDtypeStruct((1, pairs * CHANS, LAGS), jnp.bfloat16)] * count,
        in_specs=[SMEM] * 3 + [ANY] * 5,
        out_specs=[ANY] * count,
        scratch_shapes=[
            pltpu.VMEM((3, rows, width), jnp.bfloat16),
            pltpu.VMEM(flags.shape, jnp.bfloat16),
            pltpu.VMEM((3 * QUAD, windows, CHANS, 128), jnp.float32),
            pltpu.VMEM((3 * QUAD, windows, CHANS, width), jnp.float32),
            pltpu.VMEM((3 * QUAD, windows, CHANS, width), jnp.float32),
            pltpu.VMEM((pairs * CHANS // 16, 16, width), jnp.bfloat16),
            pltpu.VMEM((width, LAGS), jnp.bfloat16),
            pltpu.VMEM((count, pairs * CHANS, LAGS), jnp.bfloat16),
            pltpu.SemaphoreType.DMA((5,)),
            pltpu.SemaphoreType.DMA((count,)),
        ],
        compiler_params=pltpu.CompilerParams(vmem_limit_bytes=VMEM_BYTES),
        cost_estimate=cost(CROSS_US * count),
        name="cross_stack",
    )(meta, place, filled, *blocks, flags, lagmap)


def place_kernel(slot, r0, r1, r2, r3, *refs):
    out = refs[-1]
    for m, r in enumerate((r0, r1, r2, r3)):
        at = pl.multiple_of(slot[m] % 2 * CHANS, CHANS)
        chip = slot[m] // 2
        for p in range(0, out.shape[0], 2):
            wide = r[0, 0, pl.ds(p * CHANS, 2 * CHANS), :].astype(jnp.float32)
            out[p, chip, pl.ds(at, CHANS), :] = wide[:CHANS]
            out[p + 1, chip, pl.ds(at, CHANS), :] = wide[CHANS:]


def place_stacks(first, slot, parts, held, shape):
    extra = [] if held is None else [held]
    step = 8
    depth = parts[0].shape[0]
    parts = [part.reshape(depth, 2, -1, LAGS) for part in parts]
    spot = [
        pl.BlockSpec((1, 1, step * CHANS, LAGS), lambda c, i, *_, k=k: (c, k, i, 0))
        for k in (0, 0, 1, 1)
    ]
    return pl.pallas_call(
        place_kernel,
        out_shape=jax.ShapeDtypeStruct(shape, jnp.float32),
        grid_spec=pltpu.PrefetchScalarGridSpec(
            num_scalar_prefetch=1,
            grid=(depth, shape[0] // step),
            in_specs=spot + [ANY] * len(extra),
            out_specs=pl.BlockSpec(
                (step, 2, 2 * CHANS, LAGS), lambda c, i, *_: (i, 0, first + c, 0)
            ),
        ),
        input_output_aliases={5: 0} if extra else {},
        compiler_params=pltpu.CompilerParams(vmem_limit_bytes=VMEM_BYTES),
        cost_estimate=cost(PLACE_US * depth),
        name="place_stacks",
    )(slot, *parts, *extra)


def body(records, dead, glitch, pairs):
    windows, block, width = records.shape
    bins = width // 2
    slots = pairs.shape[0]
    half = block // 2
    wide = 2 * CHANS
    chunks = half // wide
    here = lax.axis_index("chan")
    mine = here % QUAD
    quad = here // QUAD
    chip = mine // 2
    meta = jnp.stack([mine % 2, chip * half]).astype(jnp.int32)
    basis = jnp.asarray(make_basis(width, bins))
    hann = jnp.asarray(make_hann(width))
    lagmap = jnp.asarray(make_lagmap(width, bins, LAGS))
    core = mine % 2
    split = records.reshape(windows, 2, chunks, 2, CHANS, width)

    def cut(c, count, core):
        start = (0, 1 - chip, c, core, 0, 0)
        sizes = (windows, 1, count, 1, CHANS, width)
        return lax.dynamic_slice(split, start, sizes).reshape(-1, width)

    def exchange(c, count, core, *pages):
        near_core = jnp.concatenate([cut(c, count, core), *pages])
        far_core = jnp.concatenate([cut(c, count, 1 - core), *pages])
        near_core, far_core = lax.optimization_barrier((near_core, far_core))
        n = len(got)
        got.append(
            (to_quad_peer(near_core, 2, f"Y{n}A_"), to_quad_peer(far_core, 3, f"Y{n}B_"))
        )
        return near_core

    got = []
    sent = exchange(0, 1, core)
    core = after(core, sent)
    own_peer = to_quad_peer(records, 1, "CA_")
    live = after((dead[None, :] * glitch).astype(jnp.bfloat16), sent)
    columns = [swap_quads(live, 0, "NE_"), live, swap_quads(live, 1, "NO_")]
    columns.append(jnp.pad(pairs.astype(jnp.bfloat16), ((0, 0), (0, block - 2))))
    page = jnp.concatenate([jnp.pad(x, ((0, 16 - x.shape[0]), (0, 0))) for x in columns], 1)
    page = jnp.pad(page, ((0, 0), (0, width - page.shape[1])))
    exchange(1, 1, core, page)
    white, near = [], []

    def whiten_next(c, count, *earlier):
        mate = after(meta, *earlier)
        for w in whiten(c * wide, count, mate, records, got[c][0], own_peer, got[c][1], hann, basis):
            n = len(white)
            near.append((swap_quads(w, 0, f"Z{n}E_"), w, swap_quads(w, 1, f"Z{n}O_")))
            white.append(w)

    whiten_next(0, 1)
    exchange(2, chunks - 2, after(core, white[0]))
    notes_peer = to_quad_peer(after(page, white[0]), 1, "NC_")
    whiten_next(1, 1, notes_peer)
    whiten_next(2, chunks - 2, white[1])
    pages = [after(part, white[1])[-16:] for part in got[1]]
    notes = jnp.stack([page, pages[0], notes_peer, pages[1]])
    flags = notes[:, :windows, : 3 * block].reshape(QUAD, windows, 3, block)
    flags = flags.transpose(2, 0, 1, 3).reshape(-1, block)

    listed = notes[:, :slots, 3 * block : 3 * block + 2].astype(jnp.int32)
    listed = listed.reshape(2, 2, slots, 2)
    listed = listed.swapaxes(0, 1)[::-1].reshape(-1, 2)
    filled = (listed[..., 0] >= 0) & (listed[..., 1] >= 0)
    inside = (listed % QUAD) ^ mine
    side = jnp.where(quad % 2 == 0, 1, -1)
    place = (1 - (listed // QUAD - quad) * side) * QUAD + (inside % 2) * 2 + inside // 2
    place = jnp.where(filled[..., None], jnp.clip(place, 0, 3 * QUAD - 1), 0)
    filled = filled.astype(jnp.int32)
    slot = jnp.stack([mine ^ m for m in MASKS]).astype(jnp.int32)
    shape = (slots, 2, half, LAGS)

    def cross(sides, c, place):
        return cross_stack(sides, c, windows, meta, place, filled, near[c], flags, lagmap)

    def returned(home, away, name):
        return (
            home,
            away,
            to_quad_peer(home, 1, "H" + name),
            to_quad_peer(away, 1, "F" + name),
        )

    held, sent = None, None
    place = after(place, *white)
    for c in range(chunks - 1):
        away, home = cross((0, 1), c, place)
        if sent:
            held = place_stacks(c - 1, slot, returned(*after(sent, home), str(c - 1) + "_"), held, shape)
        place = after(place, home if held is None else held)
        sent = (home, to_quad_peer(away, 2, f"R{c}_"))
    c = chunks - 1
    (away,) = cross((0,), c, place)
    held = place_stacks(c - 1, slot, returned(*after(sent, away), str(c - 1) + "_"), held, shape)
    away = to_quad_peer(away, 2, f"R{c}_")
    (home,) = cross((1,), c, after(place, held))
    held = place_stacks(c, slot, returned(home, away, str(c) + "_"), held, shape)
    return held.reshape(slots, block, LAGS)


def solution(mesh):
    placed = (
        P(None, ("group", "chan"), None),
        P(("group", "chan")),
        P(None, ("group", "chan")),
        P(("group", "chan"), None),
    )
    return jax.shard_map(
        body,
        mesh=mesh,
        in_specs=placed,
        out_specs=P(("group", "chan"), None, None),
        check_vma=False,
    )
```
